768 devices in a mesh: wave: 48 (over x, z), lat: 16 (over y, core).
Axes of the slice: x: 4, y: 8, z: 12, core: 2. Of those that a mesh axis runs over, the one named last changes fastest.
Arguments:
- legendre: bfloat16 [384, 384, 1536], P('wave', None, 'lat'), may hold values from -0.3125 to 0.3125
- coefficients: bfloat16 [384, 384, 128], P('wave', 'lat'), may hold values from -0.29882812 to 0.29882812
- assignment: int32 [384], replicated, may hold values from 0 to 383, as said below
Outputs:
- grid: float32 [16, 96, 64, 5120], P('lat', 'wave')
The draws below stay inside these ranges and needn't reach their ends.
Inputs may be any that keep to these rules, and one draw needn't show every extreme that they name: assignment is a permutation of the 384 slab indices; storage rows 2 i and 2 i + 1 hold slab indices j and 383 - j.
All inputs are finite; a program needn't handle non-finite values.
Results may differ from the reference program's by a relative error of at most 0.0037.
Values may be sent and summed in bfloat16 or wider, within the bound.
No kernel may reach another device: no remote copies, remote signals or barrier semaphores. Data moves between devices by JAX's collectives and lax.ppermute only.
A program may use at most 64 MiB of HBM per device.

```python
import jax
import jax.numpy as jnp
from jax import lax

M = 384
K = 384
MTOP = 2559
C = 64
LONGITUDES = 5120
LAT_DEV = 96
LAT_BLOCKS = 16
NLAT = 1536


def draw_assignment(key, part):
    key = jax.random.fold_in(key, 7)
    pair_order = jax.random.permutation(key, M // 2).astype(jnp.int32)
    return jnp.stack([pair_order, M - 1 - pair_order], axis=1).reshape(M).astype(jnp.int32)


def steps_of(stream_key, dims, shards, low, high):
    gain = 1.0
    for dim, blocks in shards:
        draws = jax.random.uniform(jax.random.fold_in(jax.random.fold_in(stream_key, 6), dim), (blocks,), jnp.float32, low / len(shards), high / len(shards))
        gain = gain * jnp.repeat(jnp.exp(draws), dims[dim] // blocks).reshape((-1,) + (1,) * (len(dims) - 1 - dim))
    return gain


def centred(rng, extent, width, reach, pieces=(), kind=jnp.bfloat16):
    array = jax.random.normal(rng, extent, jnp.float32) * width
    if len(pieces) > 0:
        array = steps_of(rng, extent, pieces, -0.22, 0.18) * array
    return jnp.clip(array, min=-reach, max=reach).astype(kind)


def setup_inputs(seed: int = 0) -> dict:
    streams_of = jax.random.split(jax.random.key(seed), 4)
    legendre = centred(streams_of[0], (M, K, NLAT), K ** -0.5, 0.3125, ((0, 48), (2, 16)))
    coefficients = centred(streams_of[1], (M, K, 2 * C), 0.05, 0.29882812, ((0, 48), (1, 16)))
    assignment = draw_assignment(jax.random.fold_in(streams_of[3], 71), 0)
    return dict(legendre=legendre, coefficients=coefficients, assignment=assignment)


def build_table(assignment, all_rows):
    table_row = jnp.arange(2 * all_rows, dtype=jnp.int32)
    frequency = (MTOP - all_rows + 1 + assignment[table_row // 2]).astype(jnp.int32)
    longitude = jnp.arange(LONGITUDES, dtype=jnp.int32)
    phase_index = (frequency[:, None] * longitude[None, :]) % LONGITUDES
    angles = phase_index.astype(jnp.float32) * jnp.float32(2.0 * 3.141592653589793 / LONGITUDES)
    parity = (table_row % 2)[:, None] == 0
    dft_table = jnp.where(parity, 2.0 * jnp.cos(angles), -2.0 * jnp.sin(angles))
    return dft_table.astype(jnp.bfloat16)


def reference(legendre, coefficients, assignment):
    all_rows = assignment.shape[0]
    degree = jnp.arange(K, dtype=jnp.int32)
    keep_mask = degree[None, :] < (all_rows - assignment)[:, None]
    masked = jnp.where(keep_mask[:, :, None], coefficients, jnp.zeros_like(coefficients))
    masked_wide = masked.astype(jnp.float32)
    dft_table = build_table(assignment, all_rows).astype(jnp.float32)

    def one_block(block_index):
        table_part = lax.dynamic_slice_in_dim(legendre, block_index * LAT_DEV, LAT_DEV, 2).astype(jnp.float32)
        fields = jnp.einsum("rkl,rkc->lrc", table_part, masked_wide).astype(jnp.bfloat16)
        spectra_rows = fields.reshape(LAT_DEV, all_rows * 2, C).astype(jnp.float32)
        return jnp.einsum("imc,mn->icn", spectra_rows, dft_table)

    return lax.map(one_block, jnp.arange(LAT_BLOCKS, dtype=jnp.int32))
```

```python
import jax
import jax.numpy as jnp
from jax import lax
from jax.experimental import pallas as pl
from jax.experimental.pallas import tpu as pltpu
from jax.sharding import PartitionSpec as P

MTOP = 2559
C = 64
LONGITUDES = 5120
QUARTER = LONGITUDES // 4
LANES = 128
CHUNK = 256


def cos_sin_of_index(index):
    turn = jnp.floor((index + 0.5 * QUARTER) * (1.0 / QUARTER))
    rest = index - turn * QUARTER
    t = rest * (2.0 * 3.141592653589793 / LONGITUDES)
    t2 = t * t
    sin = t + t * t2 * (-1.6666667e-1 + t2 * (8.3333310e-3 + t2 * (-1.9840874e-4 + t2 * 2.7525562e-6)))
    cos = 1.0 + t2 * (-0.5 + t2 * (4.16666418e-2 + t2 * (-1.38888434e-3 + t2 * 2.47609e-5)))
    quadrant = turn - 4.0 * jnp.floor(turn * 0.25)
    odd = (quadrant == 1.0) | (quadrant == 3.0)
    cos_out = jnp.where(odd, sin, cos)
    sin_out = jnp.where(odd, cos, sin)
    cos_out = jnp.where((quadrant == 1.0) | (quadrant == 2.0), -cos_out, cos_out)
    sin_out = jnp.where(quadrant >= 2.0, -sin_out, sin_out)
    return cos_out, sin_out


def table_kernel(first, assignment_ref, table_ref):
    rows = assignment_ref.shape[1]
    slab = jnp.broadcast_to(assignment_ref[...], (LANES, rows)).astype(jnp.float32).T
    frequency = slab + float(first)
    lane = lax.broadcasted_iota(jnp.int32, (rows, LANES), 1).astype(jnp.float32)
    cos, sin = cos_sin_of_index(frequency * lane)
    step_cos, step_sin = cos_sin_of_index(frequency * float(LANES))
    cos, sin = 2.0 * cos, -2.0 * sin
    for block in range(QUARTER // LANES):
        columns = slice(block * LANES, (block + 1) * LANES)
        table_ref[:rows, columns] = cos.astype(table_ref.dtype)
        table_ref[rows:, columns] = sin.astype(table_ref.dtype)
        if block + 1 < QUARTER // LANES:
            cos, sin = cos * step_cos + sin * step_sin, sin * step_cos - cos * step_sin


def build_table(assignment):
    rows = assignment.shape[0]
    return pl.pallas_call(
        lambda a, t: table_kernel(MTOP - rows + 1, a, t),
        out_shape=jax.ShapeDtypeStruct((2 * rows, QUARTER), jnp.bfloat16),
        cost_estimate=pl.CostEstimate(flops=2 * 10 ** 9, bytes_accessed=2 * rows * QUARTER * 2, transcendentals=0),
        compiler_params=pltpu.CompilerParams(vmem_limit_bytes=16 * 2 ** 20),
        name="dft_table",
    )(assignment.reshape(1, rows))


def synthesis_kernel(first, assignment_ref, spectra_ref, table_ref, out_ref, lhs, buffer, semaphore):
    rows = assignment_ref.shape[1]
    items = spectra_ref.shape[0]
    quarter_turns = jnp.broadcast_to(assignment_ref[...], (LANES, rows)).T + first
    low = [spectra_ref[i].reshape(rows, 2 * C).astype(jnp.float32) for i in range(items)]
    real = jnp.concatenate([x[:, :C] for x in low], axis=1)
    imag = jnp.concatenate([x[:, C:] for x in low], axis=1)
    width = items * C
    for q in range(4):
        kind = (quarter_turns * q) % 4
        keep = jnp.where(kind == 0, 1.0, jnp.where(kind == 2, -1.0, 0.0)).astype(jnp.float32)
        swap = jnp.where(kind == 3, 1.0, jnp.where(kind == 1, -1.0, 0.0)).astype(jnp.float32)
        columns = slice(q * width, (q + 1) * width)
        lhs[:rows, columns] = (keep * real + swap * imag).astype(lhs.dtype)
        lhs[rows:, columns] = (keep * imag - swap * real).astype(lhs.dtype)
    chunks = QUARTER // CHUNK

    def copy(n, q):
        return pltpu.make_async_copy(
            buffer.at[n, q],
            out_ref.at[0, :, :, pl.ds(q * QUARTER + n * CHUNK, CHUNK)],
            semaphore.at[n, q],
        )

    for n in range(chunks):
        result = lax.dot_general(
            lhs[...], table_ref[:, n * CHUNK:(n + 1) * CHUNK],
            (((0,), (0,)), ((), ())), preferred_element_type=jnp.float32,
        )
        buffer[n] = result.reshape(4, items, C, CHUNK)
        for q in range(4):
            copy(n, q).start()
    for n in range(chunks):
        for q in range(4):
            copy(n, q).wait()


def synthesis(assignment, spectra, table):
    rows = assignment.shape[0]
    items = spectra.shape[0]
    chunks = QUARTER // CHUNK
    return pl.pallas_call(
        lambda *refs: synthesis_kernel(MTOP - rows + 1, *refs),
        out_shape=jax.ShapeDtypeStruct((1, items, C, LONGITUDES), jnp.float32),
        in_specs=[pl.BlockSpec(memory_space=pltpu.VMEM)] * 3,
        out_specs=pl.BlockSpec(memory_space=pl.ANY),
        scratch_shapes=[
            pltpu.VMEM((2 * rows, 4 * items * C), jnp.bfloat16),
            pltpu.VMEM((chunks, 4, items, C, CHUNK), jnp.float32),
            pltpu.SemaphoreType.DMA((chunks, 4)),
        ],
        cost_estimate=pl.CostEstimate(flops=10 ** 9, bytes_accessed=6 * 10 ** 6, transcendentals=0),
        compiler_params=pltpu.CompilerParams(vmem_limit_bytes=24 * 2 ** 20),
        name="synthesis",
    )(assignment.reshape(1, rows), spectra, table)


def shards(legendre, coefficients, assignment):
    row_count = legendre.shape[0]
    lat_count = legendre.shape[2]
    deg_count = coefficients.shape[1]
    all_rows = assignment.shape[0]
    wave_count = lax.axis_size("wave")
    lat_rows = lat_count // wave_count
    wave_index = lax.axis_index("wave")
    lat_index = lax.axis_index("lat")
    own_waves = lax.dynamic_slice_in_dim(assignment, wave_index * row_count, row_count)
    degree = lat_index * deg_count + jnp.arange(deg_count, dtype=jnp.int32)
    keep_mask = degree[None, :] < (all_rows - own_waves)[:, None]
    masked = jnp.where(keep_mask[:, :, None], coefficients, jnp.zeros_like(coefficients))
    lat_sum = jnp.einsum(
        "rkl,rkc->lrc",
        legendre,
        lax.all_gather(masked, "lat", axis=1, tiled=True),
        preferred_element_type=jnp.float32,
    )
    fields = lat_sum.astype(jnp.bfloat16)
    table = build_table(assignment)
    by_dest = fields.reshape(wave_count, lat_rows, row_count, fields.shape[2])
    exchanged = lax.all_to_all(by_dest, "wave", split_axis=0, concat_axis=2, tiled=True)
    spectra = exchanged.reshape(exchanged.shape[1], all_rows, 2 * C)
    return synthesis(assignment, spectra, table)


def solution(mesh):
    in_specs = (P("wave", None, "lat"), P("wave", "lat", None), P())
    out_specs = P("lat", "wave", None, None)
    return jax.shard_map(shards, mesh=mesh, in_specs=in_specs, out_specs=out_specs, check_vma=False)
```

```python
import jax
import jax.numpy as jnp
from jax import lax
from jax.experimental import pallas as pl
from jax.experimental.pallas import tpu as pltpu
from jax.sharding import PartitionSpec as P

MTOP = 2559
C = 64
LONGITUDES = 5120
QUARTER = LONGITUDES // 4
LANES = 128
CHUNK = 256
BLOCK_OF_CLASS = (0, 2, 1, 3)


def cos_sin_of_index(index):
    turn = jnp.floor((index + 0.5 * QUARTER) * (1.0 / QUARTER))
    rest = index - turn * QUARTER
    t = rest * (2.0 * 3.141592653589793 / LONGITUDES)
    t2 = t * t
    sin = t + t * t2 * (-1.6666667e-1 + t2 * (8.3333310e-3 + t2 * (-1.9840874e-4 + t2 * 2.7525562e-6)))
    cos = 1.0 + t2 * (-0.5 + t2 * (4.16666418e-2 + t2 * (-1.38888434e-3 + t2 * 2.47609e-5)))
    quadrant = turn - 4.0 * jnp.floor(turn * 0.25)
    odd = (quadrant == 1.0) | (quadrant == 3.0)
    cos_out = jnp.where(odd, sin, cos)
    sin_out = jnp.where(odd, cos, sin)
    cos_out = jnp.where((quadrant == 1.0) | (quadrant == 2.0), -cos_out, cos_out)
    sin_out = jnp.where(quadrant >= 2.0, -sin_out, sin_out)
    return cos_out, sin_out


def fields_kernel(assignment_ref, legendre_ref, coefficients_ref, out_ref):
    row_count, lat_count, deg_count = legendre_ref.shape
    all_rows = assignment_ref.shape[0]
    first_row = lax.axis_index("wave") * row_count
    degree = lax.broadcasted_iota(jnp.int32, (1, deg_count), 1)
    sums = []
    for row in range(row_count):
        kept = all_rows - assignment_ref[first_row + row]
        mask = jnp.where(degree < kept, 1.0, 0.0).astype(jnp.bfloat16)
        sums.append(jnp.dot(legendre_ref[row] * mask, coefficients_ref[row], preferred_element_type=jnp.float32))
    out = jnp.stack(sums, axis=1)
    out_ref[...] = out.reshape(out_ref.shape).astype(out_ref.dtype)


def legendre_sums(assignment, legendre, coefficients, wave_count):
    row_count, lat_count, deg_count = legendre.shape
    columns = coefficients.shape[2]
    return pl.pallas_call(
        fields_kernel,
        out_shape=jax.ShapeDtypeStruct((wave_count, lat_count // wave_count, row_count, columns), jnp.bfloat16),
        in_specs=[
            pl.BlockSpec(memory_space=pltpu.SMEM),
            pl.BlockSpec(memory_space=pltpu.VMEM),
            pl.BlockSpec(memory_space=pltpu.VMEM),
        ],
        out_specs=pl.BlockSpec(memory_space=pltpu.VMEM),
        compiler_params=pltpu.CompilerParams(vmem_limit_bytes=16 * 2 ** 20),
        name="legendre_sums",
    )(assignment, legendre, coefficients)


def tables_kernel(first, row_count, items, assignment_ref, table_ref, place_ref):
    rows = assignment_ref.shape[1]
    classes = len(BLOCK_OF_CLASS)
    padded = classes * LANES
    slab = jnp.broadcast_to(assignment_ref[...], (LANES, rows)).T
    kind = slab % classes
    block = jnp.where(kind == 1, 2, jnp.where(kind == 2, 1, kind))
    target = block * LANES + slab // classes
    lane = lax.broadcasted_iota(jnp.int32, (rows // row_count, items, row_count, LANES), 3)
    item = lax.broadcasted_iota(jnp.int32, (rows // row_count, items, row_count, LANES), 1)
    target = target.reshape(rows // row_count, 1, row_count, LANES) + item * padded - lane
    target = target.reshape(items * rows, LANES)
    for n in range(items * classes):
        place_ref[:, n * LANES:(n + 1) * LANES] = jnp.where(target == n * LANES, 1.0, 0.0).astype(place_ref.dtype)

    lane = lax.broadcasted_iota(jnp.int32, (LANES, LANES), 1).astype(jnp.float32)
    count = lax.broadcasted_iota(jnp.int32, (LANES, LANES), 0).astype(jnp.float32)
    for cls, position in enumerate(BLOCK_OF_CLASS):
        frequency = float(first + cls) + classes * count
        cos, sin = cos_sin_of_index(frequency * lane)
        step_cos, step_sin = cos_sin_of_index(frequency * float(LANES))
        cos, sin = 2.0 * cos, -2.0 * sin
        half, slot = divmod(position, 2)
        cos_rows = slice((4 * half + slot) * LANES, (4 * half + slot + 1) * LANES)
        sin_rows = slice((4 * half + slot + 2) * LANES, (4 * half + slot + 3) * LANES)
        for column in range(QUARTER // LANES):
            columns = slice(column * LANES, (column + 1) * LANES)
            table_ref[cos_rows, columns] = cos.astype(table_ref.dtype)
            table_ref[sin_rows, columns] = sin.astype(table_ref.dtype)
            if column + 1 < QUARTER // LANES:
                cos, sin = cos * step_cos + sin * step_sin, sin * step_cos - cos * step_sin


def build_tables(assignment, row_count, items):
    rows = assignment.shape[0]
    padded = len(BLOCK_OF_CLASS) * LANES
    return pl.pallas_call(
        lambda *refs: tables_kernel(MTOP - rows + 1, row_count, items, *refs),
        out_shape=(
            jax.ShapeDtypeStruct((2 * padded, QUARTER), jnp.bfloat16),
            jax.ShapeDtypeStruct((items * rows, items * padded), jnp.bfloat16),
        ),
        in_specs=[pl.BlockSpec(memory_space=pltpu.VMEM)],
        out_specs=(pl.BlockSpec(memory_space=pltpu.VMEM), pl.BlockSpec(memory_space=pltpu.VMEM)),
        cost_estimate=pl.CostEstimate(flops=2 * 10 ** 9, bytes_accessed=5 * 10 ** 6, transcendentals=0),
        compiler_params=pltpu.CompilerParams(vmem_limit_bytes=20 * 2 ** 20),
        name="dft_tables",
    )(assignment.reshape(1, rows))


def synthesis_kernel(items, spectra_ref, place_ref, table_ref, out_ref, buffer, semaphore):
    padded = len(BLOCK_OF_CLASS) * LANES
    placed = lax.dot_general(
        spectra_ref[...], place_ref[...], (((0,), (0,)), ((), ())), preferred_element_type=jnp.float32
    ).astype(jnp.bfloat16)

    def part(half, item, block):
        return placed[half * C:(half + 1) * C, item * padded + block * LANES:item * padded + (block + 1) * LANES]

    def rows_of(blocks):
        return jnp.concatenate([jnp.concatenate([f(i) for f in blocks], axis=1) for i in range(items)], axis=0)

    even = jnp.concatenate([
        rows_of([lambda i: part(0, i, 0), lambda i: part(0, i, 1), lambda i: part(1, i, 0), lambda i: part(1, i, 1)]),
        rows_of([lambda i: part(0, i, 0), lambda i: -part(0, i, 1), lambda i: part(1, i, 0), lambda i: -part(1, i, 1)]),
    ], axis=0)
    odd = jnp.concatenate([
        rows_of([lambda i: part(0, i, 2), lambda i: part(0, i, 3), lambda i: part(1, i, 2), lambda i: part(1, i, 3)]),
        rows_of([lambda i: -part(1, i, 2), lambda i: part(1, i, 3), lambda i: part(0, i, 2), lambda i: -part(0, i, 3)]),
    ], axis=0)
    chunks = QUARTER // CHUNK

    def copy(n, q):
        return pltpu.make_async_copy(
            buffer.at[n, q],
            out_ref.at[0, :, :, pl.ds(q * QUARTER + n * CHUNK, CHUNK)],
            semaphore.at[n, q],
        )

    for n in range(chunks):
        columns = slice(n * CHUNK, (n + 1) * CHUNK)
        from_even = jnp.dot(even, table_ref[:padded, columns], preferred_element_type=jnp.float32)
        from_odd = jnp.dot(odd, table_ref[padded:, columns], preferred_element_type=jnp.float32)
        buffer[n, :2] = (from_even + from_odd).reshape(2, items, C, CHUNK)
        buffer[n, 2:] = (from_even - from_odd).reshape(2, items, C, CHUNK)
        for q in range(4):
            copy(n, q).start()
    for n in range(chunks):
        for q in range(4):
            copy(n, q).wait()


def synthesis(spectra, place, table, items):
    chunks = QUARTER // CHUNK
    return pl.pallas_call(
        lambda *refs: synthesis_kernel(items, *refs),
        out_shape=jax.ShapeDtypeStruct((1, items, C, LONGITUDES), jnp.float32),
        in_specs=[pl.BlockSpec(memory_space=pltpu.VMEM)] * 3,
        out_specs=pl.BlockSpec(memory_space=pl.ANY),
        scratch_shapes=[
            pltpu.VMEM((chunks, 4, items, C, CHUNK), jnp.float32),
            pltpu.SemaphoreType.DMA((chunks, 4)),
        ],
        cost_estimate=pl.CostEstimate(flops=10 ** 9, bytes_accessed=6 * 10 ** 6, transcendentals=0),
        compiler_params=pltpu.CompilerParams(vmem_limit_bytes=24 * 2 ** 20),
        name="synthesis",
    )(spectra, place, table)


def shards(legendre, coefficients, assignment):
    row_count = legendre.shape[0]
    all_rows = assignment.shape[0]
    wave_count = lax.axis_size("wave")
    items = legendre.shape[2] // wave_count
    gathered = lax.all_gather(coefficients, "lat", axis=1, tiled=True)
    by_dest = legendre_sums(assignment, jnp.swapaxes(legendre, 1, 2), gathered, wave_count)
    exchanged = lax.all_to_all(by_dest, "wave", split_axis=0, concat_axis=0, tiled=True)
    table, place = build_tables(assignment, row_count, items)
    return synthesis(exchanged.reshape(items * all_rows, 2 * C), place, table, items)


def solution(mesh):
    in_specs = (P("wave", None, "lat"), P("wave", "lat", None), P())
    out_specs = P("lat", "wave", None, None)
    return jax.shard_map(shards, mesh=mesh, in_specs=in_specs, out_specs=out_specs, check_vma=False)
```

```python
import jax
import jax.numpy as jnp
import numpy as np
from jax import lax
from jax.experimental import pallas as pl
from jax.experimental.pallas import tpu as pltpu
from jax.sharding import PartitionSpec as P

MTOP = 2559
C = 64
LONGITUDES = 5120
QUARTER = LONGITUDES // 4
LANES = 128
CHUNK = 256
BLOCK_OF_CLASS = (0, 2, 1, 3)


def synthesis_table(first, rows):
    classes = len(BLOCK_OF_CLASS)
    table = np.zeros((2 * classes, LANES, QUARTER), np.float32)
    for cls, position in enumerate(BLOCK_OF_CLASS):
        frequency = first + np.arange(cls, rows, classes)
        phase = (frequency[:, None] * np.arange(QUARTER)[None, :]) % LONGITUDES
        angle = phase * (2.0 * np.pi / LONGITUDES)
        half, slot = divmod(position, 2)
        table[4 * half + slot, :len(frequency)] = 2.0 * np.cos(angle)
        table[4 * half + slot + 2, :len(frequency)] = -2.0 * np.sin(angle)
    return jnp.asarray(table.reshape(-1, QUARTER).astype(jnp.bfloat16))


def degrees_kernel(out_ref):
    out_ref[...] = lax.broadcasted_iota(jnp.int32, out_ref.shape, 1)


def degree_row(count):
    return pl.pallas_call(
        degrees_kernel,
        out_shape=jax.ShapeDtypeStruct((1, count), jnp.int32),
        out_specs=pl.BlockSpec(memory_space=pltpu.VMEM),
        cost_estimate=pl.CostEstimate(flops=10 ** 9, bytes_accessed=4 * count, transcendentals=0),
        compiler_params=pltpu.CompilerParams(vmem_limit_bytes=2 ** 20),
        name="degree_row",
    )()


def fields_kernel(assignment_ref, degree_ref, legendre_ref, coefficients_ref, out_ref, place_ref, by_latitude):
    row_count, lat_count, deg_count = legendre_ref.shape
    all_rows = assignment_ref.shape[1]
    first_row = lax.axis_index("wave") * row_count
    place = lax.broadcasted_iota(jnp.int32, (1, all_rows), 1)
    degree = degree_ref[...]
    slab = assignment_ref[...]
    for row in range(row_count):
        own = jnp.sum(jnp.where(place == first_row + row, slab, 0), axis=1, keepdims=True)
        mask = jnp.where(degree < all_rows - own, 1.0, 0.0).astype(jnp.bfloat16)
        by_latitude[pl.ds(row, lat_count, stride=row_count), :] = jnp.dot(
            legendre_ref[row] * mask, coefficients_ref[row], preferred_element_type=jnp.float32
        )
    out_ref[...] = by_latitude[...].astype(out_ref.dtype).reshape(out_ref.shape)
    classes = len(BLOCK_OF_CLASS)
    slab = jnp.broadcast_to(slab, (LANES, all_rows)).T
    kind = slab % classes
    block = jnp.where(kind == 1, 2, jnp.where(kind == 2, 1, kind))
    target = block * LANES + slab // classes - lax.broadcasted_iota(jnp.int32, slab.shape, 1)
    for n in range(classes):
        place_ref[:, n * LANES:(n + 1) * LANES] = jnp.where(target == n * LANES, 1.0, 0.0).astype(place_ref.dtype)


def legendre_sums(assignment, degree, legendre, coefficients, wave_count):
    row_count, lat_count, deg_count = legendre.shape
    columns = coefficients.shape[2]
    return pl.pallas_call(
        fields_kernel,
        out_shape=(
            jax.ShapeDtypeStruct((wave_count, lat_count // wave_count, row_count, columns), jnp.bfloat16),
            jax.ShapeDtypeStruct((assignment.shape[0], len(BLOCK_OF_CLASS) * LANES), jnp.bfloat16),
        ),
        in_specs=[pl.BlockSpec(memory_space=pltpu.VMEM)] * 4,
        out_specs=(pl.BlockSpec(memory_space=pltpu.VMEM), pl.BlockSpec(memory_space=pltpu.VMEM)),
        scratch_shapes=[pltpu.VMEM((row_count * lat_count, columns), jnp.float32)],
        compiler_params=pltpu.CompilerParams(vmem_limit_bytes=16 * 2 ** 20),
        name="legendre_sums",
    )(assignment.reshape(1, -1), degree, legendre, coefficients)


def synthesis_kernel(spectra_ref, place_ref, table_ref, out_ref, buffer, semaphore):
    items = spectra_ref.shape[1]
    rows, padded = place_ref.shape
    placed = []
    for i in range(items):
        spectra = spectra_ref[:, i].astype(jnp.float32).reshape(rows, 2 * C).astype(jnp.bfloat16)
        placed.append(lax.dot_general(
            spectra, place_ref[...], (((0,), (0,)), ((), ())), preferred_element_type=jnp.float32
        ).astype(jnp.bfloat16))

    def part(half, item, block):
        return placed[item][half * C:(half + 1) * C, block * LANES:(block + 1) * LANES]

    def rows_of(blocks):
        return jnp.concatenate([jnp.concatenate([f(i) for f in blocks], axis=1) for i in range(items)], axis=0)

    even = jnp.concatenate([
        rows_of([lambda i: part(0, i, 0), lambda i: part(0, i, 1), lambda i: part(1, i, 0), lambda i: part(1, i, 1)]),
        rows_of([lambda i: part(0, i, 0), lambda i: -part(0, i, 1), lambda i: part(1, i, 0), lambda i: -part(1, i, 1)]),
    ], axis=0)
    odd = jnp.concatenate([
        rows_of([lambda i: part(0, i, 2), lambda i: part(0, i, 3), lambda i: part(1, i, 2), lambda i: part(1, i, 3)]),
        rows_of([lambda i: -part(1, i, 2), lambda i: part(1, i, 3), lambda i: part(0, i, 2), lambda i: -part(0, i, 3)]),
    ], axis=0)
    chunks = QUARTER // CHUNK

    def copy(n, q):
        return pltpu.make_async_copy(
            buffer.at[n, q],
            out_ref.at[0, :, :, pl.ds(q * QUARTER + n * CHUNK, CHUNK)],
            semaphore.at[n, q],
        )

    for n in range(chunks):
        columns = slice(n * CHUNK, (n + 1) * CHUNK)
        from_even = jnp.dot(even, table_ref[:padded, columns], preferred_element_type=jnp.float32)
        from_odd = jnp.dot(odd, table_ref[padded:, columns], preferred_element_type=jnp.float32)
        buffer[n, :2] = (from_even + from_odd).reshape(2, items, C, CHUNK)
        buffer[n, 2:] = (from_even - from_odd).reshape(2, items, C, CHUNK)
        for q in range(4):
            copy(n, q).start()
    for n in range(chunks):
        for q in range(4):
            copy(n, q).wait()


def synthesis(spectra, place, table):
    items = spectra.shape[1]
    chunks = QUARTER // CHUNK
    return pl.pallas_call(
        synthesis_kernel,
        out_shape=jax.ShapeDtypeStruct((1, items, C, LONGITUDES), jnp.float32),
        in_specs=[pl.BlockSpec(memory_space=pltpu.VMEM)] * 3,
        out_specs=pl.BlockSpec(memory_space=pl.ANY),
        scratch_shapes=[
            pltpu.VMEM((chunks, 4, items, C, CHUNK), jnp.float32),
            pltpu.SemaphoreType.DMA((chunks, 4)),
        ],
        cost_estimate=pl.CostEstimate(flops=10 ** 9, bytes_accessed=6 * 10 ** 6, transcendentals=0),
        compiler_params=pltpu.CompilerParams(vmem_limit_bytes=24 * 2 ** 20),
        name="synthesis",
    )(spectra, place, table)


def shards(legendre, coefficients, assignment):
    wave_count = lax.axis_size("wave")
    coefficients, degree = lax.optimization_barrier((coefficients, degree_row(legendre.shape[1])))
    gathered = lax.all_gather(coefficients, "lat", axis=1, tiled=True)
    gathered, assignment = lax.optimization_barrier((gathered, assignment))
    by_dest, place = legendre_sums(assignment, degree, jnp.swapaxes(legendre, 1, 2), gathered, wave_count)
    exchanged = lax.all_to_all(by_dest, "wave", split_axis=0, concat_axis=0, tiled=True)
    table = synthesis_table(MTOP - assignment.shape[0] + 1, assignment.shape[0])
    return synthesis(exchanged, place, table)


def solution(mesh):
    in_specs = (P("wave", None, "lat"), P("wave", "lat", None), P())
    out_specs = P("lat", "wave", None, None)
    return jax.shard_map(shards, mesh=mesh, in_specs=in_specs, out_specs=out_specs, check_vma=False)
```

```python
import jax
import jax.numpy as jnp
import numpy as np
from jax import lax
from jax.experimental import pallas as pl
from jax.experimental.pallas import tpu as pltpu
from jax.sharding import PartitionSpec as P

MTOP = 2559
C = 64
LONGITUDES = 5120
QUARTER = LONGITUDES // 4
LANES = 128
CHUNK = 256
BLOCK_OF_CLASS = (0, 2, 1, 3)
WAVE_FIRST = 34


def synthesis_table(first, rows):
    classes = len(BLOCK_OF_CLASS)
    table = np.zeros((2 * classes, LANES, QUARTER), np.float32)
    for cls, position in enumerate(BLOCK_OF_CLASS):
        frequency = first + np.arange(cls, rows, classes)
        phase = (frequency[:, None] * np.arange(QUARTER)[None, :]) % LONGITUDES
        angle = phase * (2.0 * np.pi / LONGITUDES)
        half, slot = divmod(position, 2)
        table[4 * half + slot, :len(frequency)] = 2.0 * np.cos(angle)
        table[4 * half + slot + 2, :len(frequency)] = -2.0 * np.sin(angle)
    return jnp.asarray(table.reshape(-1, QUARTER).astype(jnp.bfloat16))


def degrees_kernel(_, out_ref):
    out_ref[...] = lax.broadcasted_iota(jnp.int32, out_ref.shape, 1)


def degree_row(count, after):
    return pl.pallas_call(
        degrees_kernel,
        out_shape=jax.ShapeDtypeStruct((1, count), jnp.int32),
        in_specs=[pl.BlockSpec(memory_space=pl.ANY)],
        out_specs=pl.BlockSpec(memory_space=pltpu.VMEM),
        cost_estimate=pl.CostEstimate(flops=10 ** 9, bytes_accessed=4 * count, transcendentals=0),
        compiler_params=pltpu.CompilerParams(vmem_limit_bytes=2 ** 20),
        name="degree_row",
    )(after)


def wave_order(count):
    return [(WAVE_FIRST + i) % count for i in range(count)]


def fields_kernel(assignment_ref, degree_ref, legendre_ref, coefficients_ref, out_ref, place_ref, by_latitude):
    row_count, lat_count, deg_count = legendre_ref.shape
    all_rows = assignment_ref.shape[1]
    first_row = lax.axis_index("wave") * row_count
    place = lax.broadcasted_iota(jnp.int32, (1, all_rows), 1)
    degree = degree_ref[...]
    slab = assignment_ref[...]
    for row in range(row_count):
        own = jnp.sum(jnp.where(place == first_row + row, slab, 0), axis=1, keepdims=True)
        mask = jnp.where(degree < all_rows - own, 1.0, 0.0).astype(jnp.bfloat16)
        by_latitude[pl.ds(row, lat_count, stride=row_count), :] = jnp.dot(
            legendre_ref[row] * mask, coefficients_ref[row], preferred_element_type=jnp.float32
        )
    wave_count, size = out_ref.shape[:2]
    order = wave_order(wave_count)
    for block, wave in enumerate(order):
        out_ref[block] = by_latitude[wave * size:(wave + 1) * size, :].astype(out_ref.dtype)
    classes = len(BLOCK_OF_CLASS)
    slab = jnp.broadcast_to(slab, (LANES, all_rows)).T
    slab = jnp.concatenate([slab[wave * row_count:(wave + 1) * row_count] for wave in order], axis=0)
    kind = slab % classes
    block = jnp.where(kind == 1, 2, jnp.where(kind == 2, 1, kind))
    target = block * LANES + slab // classes - lax.broadcasted_iota(jnp.int32, slab.shape, 1)
    for n in range(classes):
        place_ref[:, n * LANES:(n + 1) * LANES] = jnp.where(target == n * LANES, 1.0, 0.0).astype(place_ref.dtype)


def legendre_sums(assignment, degree, legendre, coefficients, wave_count):
    row_count, lat_count, deg_count = legendre.shape
    columns = coefficients.shape[2]
    return pl.pallas_call(
        fields_kernel,
        out_shape=(
            jax.ShapeDtypeStruct((wave_count, lat_count // wave_count * row_count, columns), jnp.bfloat16),
            jax.ShapeDtypeStruct((assignment.shape[0], len(BLOCK_OF_CLASS) * LANES), jnp.bfloat16),
        ),
        in_specs=[pl.BlockSpec(memory_space=pltpu.VMEM)] * 4,
        out_specs=(pl.BlockSpec(memory_space=pltpu.VMEM), pl.BlockSpec(memory_space=pltpu.VMEM)),
        scratch_shapes=[pltpu.VMEM((row_count * lat_count, columns), jnp.float32)],
        compiler_params=pltpu.CompilerParams(vmem_limit_bytes=16 * 2 ** 20),
        name="legendre_sums",
    )(assignment.reshape(1, -1), degree, legendre, coefficients)


def synthesis_kernel(spectra_ref, place_ref, table_ref, out_ref, buffer, semaphore):
    wave_count, size = spectra_ref.shape[:2]
    rows, padded = place_ref.shape
    row_count = rows // wave_count
    items = size // row_count
    spectra = spectra_ref[...].astype(jnp.float32)
    placed = []
    for i in range(items):
        item = spectra[:, i * row_count:(i + 1) * row_count].reshape(rows, 2 * C).astype(jnp.bfloat16)
        placed.append(lax.dot_general(
            item, place_ref[...], (((0,), (0,)), ((), ())), preferred_element_type=jnp.float32
        ).astype(jnp.bfloat16))

    def part(half, item, block):
        return placed[item][half * C:(half + 1) * C, block * LANES:(block + 1) * LANES]

    def rows_of(blocks):
        return jnp.concatenate([jnp.concatenate([f(i) for f in blocks], axis=1) for i in range(items)], axis=0)

    even = jnp.concatenate([
        rows_of([lambda i: part(0, i, 0), lambda i: part(0, i, 1), lambda i: part(1, i, 0), lambda i: part(1, i, 1)]),
        rows_of([lambda i: part(0, i, 0), lambda i: -part(0, i, 1), lambda i: part(1, i, 0), lambda i: -part(1, i, 1)]),
    ], axis=0)
    odd = jnp.concatenate([
        rows_of([lambda i: part(0, i, 2), lambda i: part(0, i, 3), lambda i: part(1, i, 2), lambda i: part(1, i, 3)]),
        rows_of([lambda i: -part(1, i, 2), lambda i: part(1, i, 3), lambda i: part(0, i, 2), lambda i: -part(0, i, 3)]),
    ], axis=0)
    chunks = QUARTER // CHUNK

    def copy(n, q):
        return pltpu.make_async_copy(
            buffer.at[n, q],
            out_ref.at[0, :, :, pl.ds(q * QUARTER + n * CHUNK, CHUNK)],
            semaphore.at[n, q],
        )

    for n in range(chunks):
        columns = slice(n * CHUNK, (n + 1) * CHUNK)
        from_even = jnp.dot(even, table_ref[:padded, columns], preferred_element_type=jnp.float32)
        from_odd = jnp.dot(odd, table_ref[padded:, columns], preferred_element_type=jnp.float32)
        buffer[n, :2] = (from_even + from_odd).reshape(2, items, C, CHUNK)
        buffer[n, 2:] = (from_even - from_odd).reshape(2, items, C, CHUNK)
        for q in range(4):
            copy(n, q).start()
    for n in range(chunks):
        for q in range(4):
            copy(n, q).wait()


def synthesis(spectra, place, table):
    items = spectra.shape[0] * spectra.shape[1] // place.shape[0]
    chunks = QUARTER // CHUNK
    return pl.pallas_call(
        synthesis_kernel,
        out_shape=jax.ShapeDtypeStruct((1, items, C, LONGITUDES), jnp.float32),
        in_specs=[pl.BlockSpec(memory_space=pltpu.VMEM)] * 3,
        out_specs=pl.BlockSpec(memory_space=pl.ANY),
        scratch_shapes=[
            pltpu.VMEM((chunks, 4, items, C, CHUNK), jnp.float32),
            pltpu.SemaphoreType.DMA((chunks, 4)),
        ],
        cost_estimate=pl.CostEstimate(flops=10 ** 9, bytes_accessed=6 * 10 ** 6, transcendentals=0),
        compiler_params=pltpu.CompilerParams(vmem_limit_bytes=24 * 2 ** 20),
        name="synthesis",
    )(spectra, place, table)


def shards(legendre, coefficients, assignment):
    wave_count = lax.axis_size("wave")
    gathered = lax.all_gather(coefficients, "lat", axis=1, tiled=True)
    degree = degree_row(legendre.shape[1], gathered)
    degree, assignment = lax.optimization_barrier((degree, assignment))
    by_dest, place = legendre_sums(assignment, degree, jnp.swapaxes(legendre, 1, 2), gathered, wave_count)
    exchanged = lax.all_to_all(
        by_dest, "wave", split_axis=0, concat_axis=0, tiled=True, axis_index_groups=[wave_order(wave_count)]
    )
    table = synthesis_table(MTOP - assignment.shape[0] + 1, assignment.shape[0])
    return synthesis(exchanged, place, table)


def solution(mesh):
    in_specs = (P("wave", None, "lat"), P("wave", "lat", None), P())
    out_specs = P("lat", "wave", None, None)
    return jax.shard_map(shards, mesh=mesh, in_specs=in_specs, out_specs=out_specs, check_vma=False)
```

```python
import jax
import jax.numpy as jnp
import numpy as np
from jax import lax
from jax.experimental import pallas as pl
from jax.experimental.pallas import tpu as pltpu
from jax.sharding import PartitionSpec as P

MTOP = 2559
C = 64
LONGITUDES = 5120
QUARTER = LONGITUDES // 4
LANES = 128
CHUNK = 256
BLOCK_OF_CLASS = (0, 2, 1, 3)
X_ORDER = (2, 0, 3, 1)
Z_ORDER = (10, 11, 5, 6, 0, 1, 2, 3, 4, 7, 8, 9)


def synthesis_table(first, rows):
    classes = len(BLOCK_OF_CLASS)
    table = np.zeros((2 * classes, LANES, QUARTER), np.float32)
    for cls, position in enumerate(BLOCK_OF_CLASS):
        frequency = first + np.arange(cls, rows, classes)
        phase = (frequency[:, None] * np.arange(QUARTER)[None, :]) % LONGITUDES
        angle = phase * (2.0 * np.pi / LONGITUDES)
        half, slot = divmod(position, 2)
        table[4 * half + slot, :len(frequency)] = 2.0 * np.cos(angle)
        table[4 * half + slot + 2, :len(frequency)] = -2.0 * np.sin(angle)
    return jnp.asarray(table.reshape(-1, QUARTER).astype(jnp.bfloat16))


def degrees_kernel(_, out_ref):
    out_ref[...] = lax.broadcasted_iota(jnp.int32, out_ref.shape, 1)


def degree_row(count, after):
    return pl.pallas_call(
        degrees_kernel,
        out_shape=jax.ShapeDtypeStruct((1, count), jnp.int32),
        in_specs=[pl.BlockSpec(memory_space=pl.ANY)],
        out_specs=pl.BlockSpec(memory_space=pltpu.VMEM),
        cost_estimate=pl.CostEstimate(flops=10 ** 9, bytes_accessed=4 * count, transcendentals=0),
        compiler_params=pltpu.CompilerParams(vmem_limit_bytes=2 ** 20),
        name="degree_row",
    )(after)


def wave_order(count):
    order = [len(Z_ORDER) * x + z for x in X_ORDER for z in Z_ORDER]
    assert sorted(order) == list(range(count))
    return order


def fields_kernel(assignment_ref, degree_ref, legendre_ref, coefficients_ref, out_ref, place_ref, by_latitude):
    row_count, lat_count, deg_count = legendre_ref.shape
    all_rows = assignment_ref.shape[1]
    first_row = lax.axis_index("wave") * row_count
    place = lax.broadcasted_iota(jnp.int32, (1, all_rows), 1)
    degree = degree_ref[...]
    slab = assignment_ref[...]
    for row in range(row_count):
        own = jnp.sum(jnp.where(place == first_row + row, slab, 0), axis=1, keepdims=True)
        mask = jnp.where(degree < all_rows - own, 1.0, 0.0).astype(jnp.bfloat16)
        by_latitude[pl.ds(row, lat_count, stride=row_count), :] = jnp.dot(
            legendre_ref[row] * mask, coefficients_ref[row], preferred_element_type=jnp.float32
        )
    wave_count, size = out_ref.shape[:2]
    order = wave_order(wave_count)
    for block, wave in enumerate(order):
        out_ref[block] = by_latitude[wave * size:(wave + 1) * size, :].astype(out_ref.dtype)
    classes = len(BLOCK_OF_CLASS)
    slab = jnp.broadcast_to(slab, (LANES, all_rows)).T
    slab = jnp.concatenate([slab[wave * row_count:(wave + 1) * row_count] for wave in order], axis=0)
    kind = slab % classes
    block = jnp.where(kind == 1, 2, jnp.where(kind == 2, 1, kind))
    target = block * LANES + slab // classes - lax.broadcasted_iota(jnp.int32, slab.shape, 1)
    for n in range(classes):
        place_ref[:, n * LANES:(n + 1) * LANES] = jnp.where(target == n * LANES, 1.0, 0.0).astype(place_ref.dtype)


def legendre_sums(assignment, degree, legendre, coefficients, wave_count):
    row_count, lat_count, deg_count = legendre.shape
    columns = coefficients.shape[2]
    return pl.pallas_call(
        fields_kernel,
        out_shape=(
            jax.ShapeDtypeStruct((wave_count, lat_count // wave_count * row_count, columns), jnp.bfloat16),
            jax.ShapeDtypeStruct((assignment.shape[0], len(BLOCK_OF_CLASS) * LANES), jnp.bfloat16),
        ),
        in_specs=[pl.BlockSpec(memory_space=pltpu.VMEM)] * 4,
        out_specs=(pl.BlockSpec(memory_space=pltpu.VMEM), pl.BlockSpec(memory_space=pltpu.VMEM)),
        scratch_shapes=[pltpu.VMEM((row_count * lat_count, columns), jnp.float32)],
        compiler_params=pltpu.CompilerParams(vmem_limit_bytes=16 * 2 ** 20),
        name="legendre_sums",
    )(assignment.reshape(1, -1), degree, legendre, coefficients)


def synthesis_kernel(spectra_ref, place_ref, table_ref, out_ref, buffer, semaphore):
    wave_count, size = spectra_ref.shape[:2]
    rows, padded = place_ref.shape
    row_count = rows // wave_count
    items = size // row_count
    spectra = spectra_ref[...].astype(jnp.float32)
    placed = []
    for i in range(items):
        item = spectra[:, i * row_count:(i + 1) * row_count].reshape(rows, 2 * C).astype(jnp.bfloat16)
        placed.append(lax.dot_general(
            item, place_ref[...], (((0,), (0,)), ((), ())), preferred_element_type=jnp.float32
        ).astype(jnp.bfloat16))

    def part(half, item, block):
        return placed[item][half * C:(half + 1) * C, block * LANES:(block + 1) * LANES]

    def rows_of(blocks):
        return jnp.concatenate([jnp.concatenate([f(i) for f in blocks], axis=1) for i in range(items)], axis=0)

    even = jnp.concatenate([
        rows_of([lambda i: part(0, i, 0), lambda i: part(0, i, 1), lambda i: part(1, i, 0), lambda i: part(1, i, 1)]),
        rows_of([lambda i: part(0, i, 0), lambda i: -part(0, i, 1), lambda i: part(1, i, 0), lambda i: -part(1, i, 1)]),
    ], axis=0)
    odd = jnp.concatenate([
        rows_of([lambda i: part(0, i, 2), lambda i: part(0, i, 3), lambda i: part(1, i, 2), lambda i: part(1, i, 3)]),
        rows_of([lambda i: -part(1, i, 2), lambda i: part(1, i, 3), lambda i: part(0, i, 2), lambda i: -part(0, i, 3)]),
    ], axis=0)
    chunks = QUARTER // CHUNK

    def copy(n, q):
        return pltpu.make_async_copy(
            buffer.at[n, q],
            out_ref.at[0, :, :, pl.ds(q * QUARTER + n * CHUNK, CHUNK)],
            semaphore.at[n, q],
        )

    for n in range(chunks):
        columns = slice(n * CHUNK, (n + 1) * CHUNK)
        from_even = jnp.dot(even, table_ref[:padded, columns], preferred_element_type=jnp.float32)
        from_odd = jnp.dot(odd, table_ref[padded:, columns], preferred_element_type=jnp.float32)
        buffer[n, :2] = (from_even + from_odd).reshape(2, items, C, CHUNK)
        buffer[n, 2:] = (from_even - from_odd).reshape(2, items, C, CHUNK)
        for q in range(4):
            copy(n, q).start()
    for n in range(chunks):
        for q in range(4):
            copy(n, q).wait()


def synthesis(spectra, place, table):
    items = spectra.shape[0] * spectra.shape[1] // place.shape[0]
    chunks = QUARTER // CHUNK
    return pl.pallas_call(
        synthesis_kernel,
        out_shape=jax.ShapeDtypeStruct((1, items, C, LONGITUDES), jnp.float32),
        in_specs=[pl.BlockSpec(memory_space=pltpu.VMEM)] * 3,
        out_specs=pl.BlockSpec(memory_space=pl.ANY),
        scratch_shapes=[
            pltpu.VMEM((chunks, 4, items, C, CHUNK), jnp.float32),
            pltpu.SemaphoreType.DMA((chunks, 4)),
        ],
        cost_estimate=pl.CostEstimate(flops=10 ** 9, bytes_accessed=6 * 10 ** 6, transcendentals=0),
        compiler_params=pltpu.CompilerParams(vmem_limit_bytes=24 * 2 ** 20),
        name="synthesis",
    )(spectra, place, table)


def shards(legendre, coefficients, assignment):
    wave_count = lax.axis_size("wave")
    gathered = lax.all_gather(coefficients, "lat", axis=1, tiled=True)
    degree = degree_row(legendre.shape[1], gathered)
    degree, assignment = lax.optimization_barrier((degree, assignment))
    by_dest, place = legendre_sums(assignment, degree, jnp.swapaxes(legendre, 1, 2), gathered, wave_count)
    exchanged = lax.all_to_all(
        by_dest, "wave", split_axis=0, concat_axis=0, tiled=True, axis_index_groups=[wave_order(wave_count)]
    )
    table = synthesis_table(MTOP - assignment.shape[0] + 1, assignment.shape[0])
    return synthesis(exchanged, place, table)


def solution(mesh):
    in_specs = (P("wave", None, "lat"), P("wave", "lat", None), P())
    out_specs = P("lat", "wave", None, None)
    return jax.shard_map(shards, mesh=mesh, in_specs=in_specs, out_specs=out_specs, check_vma=False)
```

```python
import jax
import jax.numpy as jnp
import numpy as np
from jax import lax
from jax.experimental import pallas as pl
from jax.experimental.pallas import tpu as pltpu
from jax.sharding import PartitionSpec as P

MTOP = 2559
C = 64
LONGITUDES = 5120
QUARTER = LONGITUDES // 4
LANES = 128
CHUNK = 256
BLOCK_OF_CLASS = (0, 2, 1, 3)
X_ORDER = (2, 0, 3, 1)
Z_ORDER = (10, 11, 5, 6, 0, 1, 2, 3, 4, 7, 8, 9)


def synthesis_table(first, rows):
    classes = len(BLOCK_OF_CLASS)
    table = np.zeros((2 * classes, LANES, QUARTER), np.float32)
    for cls, position in enumerate(BLOCK_OF_CLASS):
        frequency = first + np.arange(cls, rows, classes)
        phase = (frequency[:, None] * np.arange(QUARTER)[None, :]) % LONGITUDES
        angle = phase * (2.0 * np.pi / LONGITUDES)
        half, slot = divmod(position, 2)
        table[4 * half + slot, :len(frequency)] = 2.0 * np.cos(angle)
        table[4 * half + slot + 2, :len(frequency)] = -2.0 * np.sin(angle)
    return jnp.asarray(table.reshape(-1, QUARTER).astype(jnp.bfloat16))


def degrees_kernel(_, out_ref):
    out_ref[...] = lax.broadcasted_iota(jnp.int32, out_ref.shape, 1)


def degree_row(count, after):
    return pl.pallas_call(
        degrees_kernel,
        out_shape=jax.ShapeDtypeStruct((1, count), jnp.int32),
        in_specs=[pl.BlockSpec(memory_space=pl.ANY)],
        out_specs=pl.BlockSpec(memory_space=pltpu.VMEM),
        cost_estimate=pl.CostEstimate(flops=10 ** 9, bytes_accessed=4 * count, transcendentals=0),
        compiler_params=pltpu.CompilerParams(vmem_limit_bytes=2 ** 20),
        name="degree_row",
    )(after)


def wave_order(count):
    order = [len(Z_ORDER) * x + z for x in X_ORDER for z in Z_ORDER]
    assert sorted(order) == list(range(count))
    return order


def fields_kernel(assignment_ref, degree_ref, legendre_ref, coefficients_ref, out_ref, place_ref, by_latitude):
    row_count, lat_count, deg_count = legendre_ref.shape
    all_rows = assignment_ref.shape[1]
    first_row = lax.axis_index("wave") * row_count
    row = lax.broadcasted_iota(jnp.int32, (row_count, all_rows), 0)
    place = lax.broadcasted_iota(jnp.int32, (row_count, all_rows), 1)
    slab = assignment_ref[...]
    own = jnp.sum(jnp.where(place == first_row + row, slab, 0), axis=1, keepdims=True)
    masks = jnp.where(degree_ref[...] < all_rows - own, 1.0, 0.0).astype(jnp.bfloat16)
    for row in range(row_count):
        by_latitude[pl.ds(row, lat_count, stride=row_count), :] = jnp.dot(
            legendre_ref[row] * masks[row:row + 1], coefficients_ref[row], preferred_element_type=jnp.float32
        )
    wave_count, size = out_ref.shape[:2]
    order = wave_order(wave_count)
    for block, wave in enumerate(order):
        out_ref[block] = by_latitude[wave * size:(wave + 1) * size, :].astype(out_ref.dtype)
    classes = len(BLOCK_OF_CLASS)
    kind = slab % classes
    position = jnp.where(kind == 1, 2, jnp.where(kind == 2, 1, kind))
    target = jnp.broadcast_to(position * LANES + slab // classes, (LANES, all_rows)).T
    target = jnp.concatenate([target[wave * row_count:(wave + 1) * row_count] for wave in order], axis=0)
    target -= lax.broadcasted_iota(jnp.int32, target.shape, 1)
    for n in range(classes):
        place_ref[:, n * LANES:(n + 1) * LANES] = jnp.where(target == n * LANES, 1.0, 0.0).astype(place_ref.dtype)


def legendre_sums(assignment, degree, legendre, coefficients, wave_count):
    row_count, lat_count, deg_count = legendre.shape
    columns = coefficients.shape[2]
    return pl.pallas_call(
        fields_kernel,
        out_shape=(
            jax.ShapeDtypeStruct((wave_count, lat_count // wave_count * row_count, columns), jnp.bfloat16),
            jax.ShapeDtypeStruct((assignment.shape[0], len(BLOCK_OF_CLASS) * LANES), jnp.bfloat16),
        ),
        in_specs=[pl.BlockSpec(memory_space=pltpu.VMEM)] * 4,
        out_specs=(pl.BlockSpec(memory_space=pltpu.VMEM), pl.BlockSpec(memory_space=pltpu.VMEM)),
        scratch_shapes=[pltpu.VMEM((row_count * (lat_count + 1), columns), jnp.float32)],
        compiler_params=pltpu.CompilerParams(vmem_limit_bytes=16 * 2 ** 20),
        name="legendre_sums",
    )(assignment.reshape(1, -1), degree, legendre, coefficients)


def synthesis_kernel(spectra_ref, place_ref, table_ref, out_ref, buffer, semaphore):
    wave_count, size = spectra_ref.shape[:2]
    rows, padded = place_ref.shape
    row_count = rows // wave_count
    items = size // row_count
    spectra = spectra_ref[...].astype(jnp.float32)
    placed = []
    for i in range(items):
        item = spectra[:, i * row_count:(i + 1) * row_count].reshape(rows, 2 * C).astype(jnp.bfloat16)
        placed.append(lax.dot_general(
            item, place_ref[...], (((0,), (0,)), ((), ())), preferred_element_type=jnp.float32
        ).astype(jnp.bfloat16))

    def part(half, item, block):
        return placed[item][half * C:(half + 1) * C, block * LANES:(block + 1) * LANES]

    def rows_of(blocks):
        return jnp.concatenate([jnp.concatenate([f(i) for f in blocks], axis=1) for i in range(items)], axis=0)

    even = jnp.concatenate([
        rows_of([lambda i: part(0, i, 0), lambda i: part(0, i, 1), lambda i: part(1, i, 0), lambda i: part(1, i, 1)]),
        rows_of([lambda i: part(0, i, 0), lambda i: -part(0, i, 1), lambda i: part(1, i, 0), lambda i: -part(1, i, 1)]),
    ], axis=0)
    odd = jnp.concatenate([
        rows_of([lambda i: part(0, i, 2), lambda i: part(0, i, 3), lambda i: part(1, i, 2), lambda i: part(1, i, 3)]),
        rows_of([lambda i: -part(1, i, 2), lambda i: part(1, i, 3), lambda i: part(0, i, 2), lambda i: -part(0, i, 3)]),
    ], axis=0)
    chunks = QUARTER // CHUNK

    def copy(n, q):
        return pltpu.make_async_copy(
            buffer.at[n, q],
            out_ref.at[0, :, :, pl.ds(q * QUARTER + n * CHUNK, CHUNK)],
            semaphore.at[n, q],
        )

    for n in range(chunks):
        columns = slice(n * CHUNK, (n + 1) * CHUNK)
        from_even = jnp.dot(even, table_ref[:padded, columns], preferred_element_type=jnp.float32)
        from_odd = jnp.dot(odd, table_ref[padded:, columns], preferred_element_type=jnp.float32)
        buffer[n, :2] = (from_even + from_odd).reshape(2, items, C, CHUNK)
        buffer[n, 2:] = (from_even - from_odd).reshape(2, items, C, CHUNK)
        for q in range(4):
            copy(n, q).start()
    for n in range(chunks):
        for q in range(4):
            copy(n, q).wait()


def synthesis(spectra, place, table):
    items = spectra.shape[0] * spectra.shape[1] // place.shape[0]
    chunks = QUARTER // CHUNK
    return pl.pallas_call(
        synthesis_kernel,
        out_shape=jax.ShapeDtypeStruct((1, items, C, LONGITUDES), jnp.float32),
        in_specs=[pl.BlockSpec(memory_space=pltpu.VMEM)] * 3,
        out_specs=pl.BlockSpec(memory_space=pl.ANY),
        scratch_shapes=[
            pltpu.VMEM((chunks, 4, items, C, CHUNK), jnp.float32),
            pltpu.SemaphoreType.DMA((chunks, 4)),
        ],
        cost_estimate=pl.CostEstimate(flops=10 ** 9, bytes_accessed=6 * 10 ** 6, transcendentals=0),
        compiler_params=pltpu.CompilerParams(vmem_limit_bytes=24 * 2 ** 20),
        name="synthesis",
    )(spectra, place, table)


def shards(legendre, coefficients, assignment):
    wave_count = lax.axis_size("wave")
    gathered = lax.all_gather(coefficients, "lat", axis=1, tiled=True)
    degree = degree_row(legendre.shape[1], gathered)
    degree, assignment = lax.optimization_barrier((degree, assignment))
    by_dest, place = legendre_sums(assignment, degree, jnp.swapaxes(legendre, 1, 2), gathered, wave_count)
    exchanged = lax.all_to_all(
        by_dest, "wave", split_axis=0, concat_axis=0, tiled=True, axis_index_groups=[wave_order(wave_count)]
    )
    table = synthesis_table(MTOP - assignment.shape[0] + 1, assignment.shape[0])
    return synthesis(exchanged, place, table)


def solution(mesh):
    in_specs = (P("wave", None, "lat"), P("wave", "lat", None), P())
    out_specs = P("lat", "wave", None, None)
    return jax.shard_map(shards, mesh=mesh, in_specs=in_specs, out_specs=out_specs, check_vma=False)
```

```python
import jax
import jax.numpy as jnp
import numpy as np
from jax import lax
from jax.experimental import pallas as pl
from jax.experimental.pallas import tpu as pltpu
from jax.sharding import PartitionSpec as P

MTOP = 2559
C = 64
LONGITUDES = 5120
QUARTER = LONGITUDES // 4
LANES = 128
CHUNK = 256
BLOCK_OF_CLASS = (0, 2, 1, 3)
Y_ORDER = (0, 7, 6, 5, 4, 3, 2, 1)
X_ORDER = (2, 0, 3, 1)
Z_ORDER = (10, 11, 5, 6, 0, 1, 2, 3, 4, 7, 8, 9)


def synthesis_table(first, rows):
    classes = len(BLOCK_OF_CLASS)
    table = np.zeros((2 * classes, LANES, QUARTER), np.float32)
    for cls, position in enumerate(BLOCK_OF_CLASS):
        frequency = first + np.arange(cls, rows, classes)
        phase = (frequency[:, None] * np.arange(QUARTER)[None, :]) % LONGITUDES
        angle = phase * (2.0 * np.pi / LONGITUDES)
        half, slot = divmod(position, 2)
        table[4 * half + slot, :len(frequency)] = 2.0 * np.cos(angle)
        table[4 * half + slot + 2, :len(frequency)] = -2.0 * np.sin(angle)
    return jnp.asarray(table.reshape(-1, QUARTER).astype(jnp.bfloat16))


def degrees_kernel(_, out_ref):
    out_ref[...] = lax.broadcasted_iota(jnp.int32, out_ref.shape, 1)


def degree_row(count, after):
    return pl.pallas_call(
        degrees_kernel,
        out_shape=jax.ShapeDtypeStruct((1, count), jnp.int32),
        in_specs=[pl.BlockSpec(memory_space=pl.ANY)],
        out_specs=pl.BlockSpec(memory_space=pltpu.VMEM),
        cost_estimate=pl.CostEstimate(flops=10 ** 9, bytes_accessed=4 * count, transcendentals=0),
        compiler_params=pltpu.CompilerParams(vmem_limit_bytes=2 ** 20),
        name="degree_row",
    )(after)


def wave_order(count):
    order = [len(Z_ORDER) * x + z for x in X_ORDER for z in Z_ORDER]
    assert sorted(order) == list(range(count))
    return order


def fields_kernel(assignment_ref, degree_ref, legendre_ref, coefficients_ref, out_ref, place_ref, by_latitude):
    row_count, lat_count, deg_count = legendre_ref.shape
    all_rows = assignment_ref.shape[1]
    first_row = lax.axis_index("wave") * row_count
    row = lax.broadcasted_iota(jnp.int32, (row_count, all_rows), 0)
    place = lax.broadcasted_iota(jnp.int32, (row_count, all_rows), 1)
    slab = assignment_ref[...]
    own = jnp.sum(jnp.where(place == first_row + row, slab, 0), axis=1, keepdims=True)
    masks = jnp.where(degree_ref[...] < all_rows - own, 1.0, 0.0).astype(jnp.bfloat16)
    chip_degrees = deg_count // len(Y_ORDER)
    starts = [Y_ORDER.index(y) * chip_degrees for y in range(len(Y_ORDER))]
    for row in range(row_count):
        by_latitude[pl.ds(row, lat_count, stride=row_count), :] = jnp.dot(
            legendre_ref[row] * masks[row:row + 1],
            jnp.concatenate([coefficients_ref[row, start:start + chip_degrees, :] for start in starts], axis=0),
            preferred_element_type=jnp.float32,
        )
    wave_count, size = out_ref.shape[:2]
    order = wave_order(wave_count)
    for block, wave in enumerate(order):
        out_ref[block] = by_latitude[wave * size:(wave + 1) * size, :].astype(out_ref.dtype)
    classes = len(BLOCK_OF_CLASS)
    kind = slab % classes
    position = jnp.where(kind == 1, 2, jnp.where(kind == 2, 1, kind))
    target = jnp.broadcast_to(position * LANES + slab // classes, (LANES, all_rows)).T
    target = jnp.concatenate([target[wave * row_count:(wave + 1) * row_count] for wave in order], axis=0)
    target -= lax.broadcasted_iota(jnp.int32, target.shape, 1)
    for n in range(classes):
        place_ref[:, n * LANES:(n + 1) * LANES] = jnp.where(target == n * LANES, 1.0, 0.0).astype(place_ref.dtype)


def legendre_sums(assignment, degree, legendre, coefficients, wave_count):
    row_count, lat_count, deg_count = legendre.shape
    columns = coefficients.shape[2]
    return pl.pallas_call(
        fields_kernel,
        out_shape=(
            jax.ShapeDtypeStruct((wave_count, lat_count // wave_count * row_count, columns), jnp.bfloat16),
            jax.ShapeDtypeStruct((assignment.shape[0], len(BLOCK_OF_CLASS) * LANES), jnp.bfloat16),
        ),
        in_specs=[pl.BlockSpec(memory_space=pltpu.VMEM)] * 4,
        out_specs=(pl.BlockSpec(memory_space=pltpu.VMEM), pl.BlockSpec(memory_space=pltpu.VMEM)),
        scratch_shapes=[pltpu.VMEM((row_count * (lat_count + 1), columns), jnp.float32)],
        compiler_params=pltpu.CompilerParams(vmem_limit_bytes=16 * 2 ** 20),
        name="legendre_sums",
    )(assignment.reshape(1, -1), degree, legendre, coefficients)


def synthesis_kernel(spectra_ref, place_ref, table_ref, out_ref, buffer, semaphore):
    wave_count, size = spectra_ref.shape[:2]
    rows, padded = place_ref.shape
    row_count = rows // wave_count
    items = size // row_count
    spectra = spectra_ref[...].astype(jnp.float32)
    placed = []
    for i in range(items):
        item = spectra[:, i * row_count:(i + 1) * row_count].reshape(rows, 2 * C).astype(jnp.bfloat16)
        placed.append(lax.dot_general(
            item, place_ref[...], (((0,), (0,)), ((), ())), preferred_element_type=jnp.float32
        ).astype(jnp.bfloat16))

    def part(half, item, block):
        return placed[item][half * C:(half + 1) * C, block * LANES:(block + 1) * LANES]

    def rows_of(blocks):
        return jnp.concatenate([jnp.concatenate([f(i) for f in blocks], axis=1) for i in range(items)], axis=0)

    even = jnp.concatenate([
        rows_of([lambda i: part(0, i, 0), lambda i: part(0, i, 1), lambda i: part(1, i, 0), lambda i: part(1, i, 1)]),
        rows_of([lambda i: part(0, i, 0), lambda i: -part(0, i, 1), lambda i: part(1, i, 0), lambda i: -part(1, i, 1)]),
    ], axis=0)
    odd = jnp.concatenate([
        rows_of([lambda i: part(0, i, 2), lambda i: part(0, i, 3), lambda i: part(1, i, 2), lambda i: part(1, i, 3)]),
        rows_of([lambda i: -part(1, i, 2), lambda i: part(1, i, 3), lambda i: part(0, i, 2), lambda i: -part(0, i, 3)]),
    ], axis=0)
    chunks = QUARTER // CHUNK

    def copy(n, q):
        return pltpu.make_async_copy(
            buffer.at[n, q],
            out_ref.at[0, :, :, pl.ds(q * QUARTER + n * CHUNK, CHUNK)],
            semaphore.at[n, q],
        )

    for n in range(chunks):
        columns = slice(n * CHUNK, (n + 1) * CHUNK)
        from_even = jnp.dot(even, table_ref[:padded, columns], preferred_element_type=jnp.float32)
        from_odd = jnp.dot(odd, table_ref[padded:, columns], preferred_element_type=jnp.float32)
        buffer[n, :2] = (from_even + from_odd).reshape(2, items, C, CHUNK)
        buffer[n, 2:] = (from_even - from_odd).reshape(2, items, C, CHUNK)
        for q in range(4):
            copy(n, q).start()
    for n in range(chunks):
        for q in range(4):
            copy(n, q).wait()


def synthesis(spectra, place, table):
    items = spectra.shape[0] * spectra.shape[1] // place.shape[0]
    chunks = QUARTER // CHUNK
    return pl.pallas_call(
        synthesis_kernel,
        out_shape=jax.ShapeDtypeStruct((1, items, C, LONGITUDES), jnp.float32),
        in_specs=[pl.BlockSpec(memory_space=pltpu.VMEM)] * 3,
        out_specs=pl.BlockSpec(memory_space=pl.ANY),
        scratch_shapes=[
            pltpu.VMEM((chunks, 4, items, C, CHUNK), jnp.float32),
            pltpu.SemaphoreType.DMA((chunks, 4)),
        ],
        cost_estimate=pl.CostEstimate(flops=10 ** 9, bytes_accessed=6 * 10 ** 6, transcendentals=0),
        compiler_params=pltpu.CompilerParams(vmem_limit_bytes=24 * 2 ** 20),
        name="synthesis",
    )(spectra, place, table)


def shards(legendre, coefficients, assignment):
    wave_count = lax.axis_size("wave")
    ring = [2 * y + core for y in Y_ORDER for core in range(2)]
    gathered = lax.all_gather(coefficients, "lat", axis=1, tiled=True, axis_index_groups=[ring])
    degree = degree_row(legendre.shape[1], gathered)
    degree, assignment = lax.optimization_barrier((degree, assignment))
    by_dest, place = legendre_sums(assignment, degree, jnp.swapaxes(legendre, 1, 2), gathered, wave_count)
    exchanged = lax.all_to_all(
        by_dest, "wave", split_axis=0, concat_axis=0, tiled=True, axis_index_groups=[wave_order(wave_count)]
    )
    table = synthesis_table(MTOP - assignment.shape[0] + 1, assignment.shape[0])
    return synthesis(exchanged, place, table)


def solution(mesh):
    in_specs = (P("wave", None, "lat"), P("wave", "lat", None), P())
    out_specs = P("lat", "wave", None, None)
    return jax.shard_map(shards, mesh=mesh, in_specs=in_specs, out_specs=out_specs, check_vma=False)
```

```python
import jax
import jax.numpy as jnp
import numpy as np
from jax import lax
from jax.experimental import pallas as pl
from jax.experimental.pallas import tpu as pltpu
from jax.sharding import PartitionSpec as P

MTOP = 2559
C = 64
LONGITUDES = 5120
QUARTER = LONGITUDES // 4
LANES = 128
CHUNK = 256
BLOCK_OF_CLASS = (0, 2, 1, 3)
Y_ORDER = (6, 5, 4, 3, 2, 1, 0, 7)
X_ORDER = (2, 0, 3, 1)
Z_ORDER = (10, 11, 5, 6, 0, 1, 2, 3, 4, 7, 8, 9)


def synthesis_table(first, rows):
    classes = len(BLOCK_OF_CLASS)
    table = np.zeros((2 * classes, LANES, QUARTER), np.float32)
    for cls, position in enumerate(BLOCK_OF_CLASS):
        frequency = first + np.arange(cls, rows, classes)
        phase = (frequency[:, None] * np.arange(QUARTER)[None, :]) % LONGITUDES
        angle = phase * (2.0 * np.pi / LONGITUDES)
        half, slot = divmod(position, 2)
        table[4 * half + slot, :len(frequency)] = 2.0 * np.cos(angle)
        table[4 * half + slot + 2, :len(frequency)] = -2.0 * np.sin(angle)
    return jnp.asarray(table.reshape(-1, QUARTER).astype(jnp.bfloat16))


def degrees_kernel(_, out_ref):
    out_ref[...] = lax.broadcasted_iota(jnp.int32, out_ref.shape, 1)


def degree_row(count, after):
    return pl.pallas_call(
        degrees_kernel,
        out_shape=jax.ShapeDtypeStruct((1, count), jnp.int32),
        in_specs=[pl.BlockSpec(memory_space=pl.ANY)],
        out_specs=pl.BlockSpec(memory_space=pltpu.VMEM),
        cost_estimate=pl.CostEstimate(flops=10 ** 9, bytes_accessed=4 * count, transcendentals=0),
        compiler_params=pltpu.CompilerParams(vmem_limit_bytes=2 ** 20),
        name="degree_row",
    )(after)


def wave_order(count):
    order = [len(Z_ORDER) * x + z for x in X_ORDER for z in Z_ORDER]
    assert sorted(order) == list(range(count))
    return order


def fields_kernel(assignment_ref, degree_ref, legendre_ref, coefficients_ref, out_ref, place_ref, by_latitude):
    row_count, lat_count, deg_count = legendre_ref.shape
    all_rows = assignment_ref.shape[1]
    first_row = lax.axis_index("wave") * row_count
    row = lax.broadcasted_iota(jnp.int32, (row_count, all_rows), 0)
    place = lax.broadcasted_iota(jnp.int32, (row_count, all_rows), 1)
    slab = assignment_ref[...]
    own = jnp.sum(jnp.where(place == first_row + row, slab, 0), axis=1, keepdims=True)
    masks = jnp.where(degree_ref[...] < all_rows - own, 1.0, 0.0).astype(jnp.bfloat16)
    chip_degrees = deg_count // len(Y_ORDER)
    starts = [Y_ORDER.index(y) * chip_degrees for y in range(len(Y_ORDER))]
    for row in range(row_count):
        by_latitude[pl.ds(row, lat_count, stride=row_count), :] = jnp.dot(
            legendre_ref[row] * masks[row:row + 1],
            jnp.concatenate([coefficients_ref[row, start:start + chip_degrees, :] for start in starts], axis=0),
            preferred_element_type=jnp.float32,
        )
    wave_count, size = out_ref.shape[:2]
    order = wave_order(wave_count)
    for block, wave in enumerate(order):
        out_ref[block] = by_latitude[wave * size:(wave + 1) * size, :].astype(out_ref.dtype)
    classes = len(BLOCK_OF_CLASS)
    kind = slab % classes
    position = jnp.where(kind == 1, 2, jnp.where(kind == 2, 1, kind))
    target = jnp.broadcast_to(position * LANES + slab // classes, (LANES, all_rows)).T
    target = jnp.concatenate([target[wave * row_count:(wave + 1) * row_count] for wave in order], axis=0)
    target -= lax.broadcasted_iota(jnp.int32, target.shape, 1)
    for n in range(classes):
        place_ref[:, n * LANES:(n + 1) * LANES] = jnp.where(target == n * LANES, 1.0, 0.0).astype(place_ref.dtype)


def legendre_sums(assignment, degree, legendre, coefficients, wave_count):
    row_count, lat_count, deg_count = legendre.shape
    columns = coefficients.shape[2]
    return pl.pallas_call(
        fields_kernel,
        out_shape=(
            jax.ShapeDtypeStruct((wave_count, lat_count // wave_count * row_count, columns), jnp.bfloat16),
            jax.ShapeDtypeStruct((assignment.shape[0], len(BLOCK_OF_CLASS) * LANES), jnp.bfloat16),
        ),
        in_specs=[pl.BlockSpec(memory_space=pltpu.VMEM)] * 4,
        out_specs=(pl.BlockSpec(memory_space=pltpu.VMEM), pl.BlockSpec(memory_space=pltpu.VMEM)),
        scratch_shapes=[pltpu.VMEM((row_count * (lat_count + 1), columns), jnp.float32)],
        compiler_params=pltpu.CompilerParams(vmem_limit_bytes=16 * 2 ** 20),
        name="legendre_sums",
    )(assignment.reshape(1, -1), degree, legendre, coefficients)


def synthesis_kernel(spectra_ref, place_ref, table_ref, out_ref, buffer, semaphore):
    wave_count, size = spectra_ref.shape[:2]
    rows, padded = place_ref.shape
    row_count = rows // wave_count
    items = size // row_count
    spectra = spectra_ref[...].astype(jnp.float32)
    placed = []
    for i in range(items):
        item = spectra[:, i * row_count:(i + 1) * row_count].reshape(rows, 2 * C).astype(jnp.bfloat16)
        placed.append(lax.dot_general(
            item, place_ref[...], (((0,), (0,)), ((), ())), preferred_element_type=jnp.float32
        ).astype(jnp.bfloat16))

    def part(half, item, block):
        return placed[item][half * C:(half + 1) * C, block * LANES:(block + 1) * LANES]

    def rows_of(blocks):
        return jnp.concatenate([jnp.concatenate([f(i) for f in blocks], axis=1) for i in range(items)], axis=0)

    even = jnp.concatenate([
        rows_of([lambda i: part(0, i, 0), lambda i: part(0, i, 1), lambda i: part(1, i, 0), lambda i: part(1, i, 1)]),
        rows_of([lambda i: part(0, i, 0), lambda i: -part(0, i, 1), lambda i: part(1, i, 0), lambda i: -part(1, i, 1)]),
    ], axis=0)
    odd = jnp.concatenate([
        rows_of([lambda i: part(0, i, 2), lambda i: part(0, i, 3), lambda i: part(1, i, 2), lambda i: part(1, i, 3)]),
        rows_of([lambda i: -part(1, i, 2), lambda i: part(1, i, 3), lambda i: part(0, i, 2), lambda i: -part(0, i, 3)]),
    ], axis=0)
    chunks = QUARTER // CHUNK

    def copy(n, q):
        return pltpu.make_async_copy(
            buffer.at[n, q],
            out_ref.at[0, :, :, pl.ds(q * QUARTER + n * CHUNK, CHUNK)],
            semaphore.at[n, q],
        )

    for n in range(chunks):
        columns = slice(n * CHUNK, (n + 1) * CHUNK)
        from_even = jnp.dot(even, table_ref[:padded, columns], preferred_element_type=jnp.float32)
        from_odd = jnp.dot(odd, table_ref[padded:, columns], preferred_element_type=jnp.float32)
        buffer[n, :2] = (from_even + from_odd).reshape(2, items, C, CHUNK)
        buffer[n, 2:] = (from_even - from_odd).reshape(2, items, C, CHUNK)
        for q in range(4):
            copy(n, q).start()
    for n in range(chunks):
        for q in range(4):
            copy(n, q).wait()


def synthesis(spectra, place, table):
    items = spectra.shape[0] * spectra.shape[1] // place.shape[0]
    chunks = QUARTER // CHUNK
    return pl.pallas_call(
        synthesis_kernel,
        out_shape=jax.ShapeDtypeStruct((1, items, C, LONGITUDES), jnp.float32),
        in_specs=[pl.BlockSpec(memory_space=pltpu.VMEM)] * 3,
        out_specs=pl.BlockSpec(memory_space=pl.ANY),
        scratch_shapes=[
            pltpu.VMEM((chunks, 4, items, C, CHUNK), jnp.float32),
            pltpu.SemaphoreType.DMA((chunks, 4)),
        ],
        cost_estimate=pl.CostEstimate(flops=10 ** 9, bytes_accessed=6 * 10 ** 6, transcendentals=0),
        compiler_params=pltpu.CompilerParams(vmem_limit_bytes=24 * 2 ** 20),
        name="synthesis",
    )(spectra, place, table)


def shards(legendre, coefficients, assignment):
    wave_count = lax.axis_size("wave")
    ring = [2 * y + core for y in Y_ORDER for core in range(2)]
    gathered = lax.all_gather(coefficients, "lat", axis=1, tiled=True, axis_index_groups=[ring])
    degree = degree_row(legendre.shape[1], gathered)
    degree, assignment = lax.optimization_barrier((degree, assignment))
    by_dest, place = legendre_sums(assignment, degree, jnp.swapaxes(legendre, 1, 2), gathered, wave_count)
    exchanged = lax.all_to_all(
        by_dest, "wave", split_axis=0, concat_axis=0, tiled=True, axis_index_groups=[wave_order(wave_count)]
    )
    table = synthesis_table(MTOP - assignment.shape[0] + 1, assignment.shape[0])
    return synthesis(exchanged, place, table)


def solution(mesh):
    in_specs = (P("wave", None, "lat"), P("wave", "lat", None), P())
    out_specs = P("lat", "wave", None, None)
    return jax.shard_map(shards, mesh=mesh, in_specs=in_specs, out_specs=out_specs, check_vma=False)
```

```python
import jax
import jax.numpy as jnp
import numpy as np
from jax import lax
from jax.experimental import pallas as pl
from jax.experimental.pallas import tpu as pltpu
from jax.sharding import PartitionSpec as P

MTOP = 2559
C = 64
LONGITUDES = 5120
QUARTER = LONGITUDES // 4
LANES = 128
CHUNK = 256
BLOCK_OF_CLASS = (0, 2, 1, 3)
Y_ORDER = (0, 7, 6, 5, 4, 3, 2, 1)
X_ORDER = (2, 0, 3, 1)
Z_ORDER = (5, 6, 0, 1, 2, 3, 4, 7, 8, 9, 10, 11)
FIRST = 34


def synthesis_table(first, rows):
    classes = len(BLOCK_OF_CLASS)
    table = np.zeros((2 * classes, LANES, QUARTER), np.float32)
    for cls, position in enumerate(BLOCK_OF_CLASS):
        frequency = first + np.arange(cls, rows, classes)
        phase = (frequency[:, None] * np.arange(QUARTER)[None, :]) % LONGITUDES
        angle = phase * (2.0 * np.pi / LONGITUDES)
        half, slot = divmod(position, 2)
        table[4 * half + slot, :len(frequency)] = 2.0 * np.cos(angle)
        table[4 * half + slot + 2, :len(frequency)] = -2.0 * np.sin(angle)
    return jnp.asarray(table.reshape(-1, QUARTER).astype(jnp.bfloat16))


def degrees_kernel(_, out_ref):
    out_ref[...] = lax.broadcasted_iota(jnp.int32, out_ref.shape, 1)


def degree_row(count, after):
    return pl.pallas_call(
        degrees_kernel,
        out_shape=jax.ShapeDtypeStruct((1, count), jnp.int32),
        in_specs=[pl.BlockSpec(memory_space=pl.ANY)],
        out_specs=pl.BlockSpec(memory_space=pltpu.VMEM),
        cost_estimate=pl.CostEstimate(flops=10 ** 9, bytes_accessed=4 * count, transcendentals=0),
        compiler_params=pltpu.CompilerParams(vmem_limit_bytes=2 ** 20),
        name="degree_row",
    )(after)


def wave_order(count):
    order = [len(Z_ORDER) * x + z for x in X_ORDER for z in Z_ORDER]
    order = order[order.index(FIRST):] + order[:order.index(FIRST)]
    assert sorted(order) == list(range(count))
    return order


def fields_kernel(assignment_ref, degree_ref, legendre_ref, coefficients_ref, out_ref, place_ref, by_latitude):
    row_count, lat_count, deg_count = legendre_ref.shape
    all_rows = assignment_ref.shape[1]
    first_row = lax.axis_index("wave") * row_count
    row = lax.broadcasted_iota(jnp.int32, (row_count, all_rows), 0)
    place = lax.broadcasted_iota(jnp.int32, (row_count, all_rows), 1)
    slab = assignment_ref[...]
    own = jnp.sum(jnp.where(place == first_row + row, slab, 0), axis=1, keepdims=True)
    masks = jnp.where(degree_ref[...] < all_rows - own, 1.0, 0.0).astype(jnp.bfloat16)
    chip_degrees = deg_count // len(Y_ORDER)
    starts = [Y_ORDER.index(y) * chip_degrees for y in range(len(Y_ORDER))]
    for row in range(row_count):
        by_latitude[pl.ds(row, lat_count, stride=row_count), :] = jnp.dot(
            legendre_ref[row] * masks[row:row + 1],
            jnp.concatenate([coefficients_ref[row, start:start + chip_degrees, :] for start in starts], axis=0),
            preferred_element_type=jnp.float32,
        )
    wave_count, size = out_ref.shape[:2]
    order = wave_order(wave_count)
    for block, wave in enumerate(order):
        out_ref[block] = by_latitude[wave * size:(wave + 1) * size, :].astype(out_ref.dtype)
    classes = len(BLOCK_OF_CLASS)
    kind = slab % classes
    position = jnp.where(kind == 1, 2, jnp.where(kind == 2, 1, kind))
    target = jnp.broadcast_to(position * LANES + slab // classes, (LANES, all_rows)).T
    target = jnp.concatenate([target[wave * row_count:(wave + 1) * row_count] for wave in order], axis=0)
    target -= lax.broadcasted_iota(jnp.int32, target.shape, 1)
    for n in range(classes):
        place_ref[:, n * LANES:(n + 1) * LANES] = jnp.where(target == n * LANES, 1.0, 0.0).astype(place_ref.dtype)


def legendre_sums(assignment, degree, legendre, coefficients, wave_count):
    row_count, lat_count, deg_count = legendre.shape
    columns = coefficients.shape[2]
    return pl.pallas_call(
        fields_kernel,
        out_shape=(
            jax.ShapeDtypeStruct((wave_count, lat_count // wave_count * row_count, columns), jnp.bfloat16),
            jax.ShapeDtypeStruct((assignment.shape[0], len(BLOCK_OF_CLASS) * LANES), jnp.bfloat16),
        ),
        in_specs=[pl.BlockSpec(memory_space=pltpu.VMEM)] * 4,
        out_specs=(pl.BlockSpec(memory_space=pltpu.VMEM), pl.BlockSpec(memory_space=pltpu.VMEM)),
        scratch_shapes=[pltpu.VMEM((row_count * (lat_count + 1), columns), jnp.float32)],
        compiler_params=pltpu.CompilerParams(vmem_limit_bytes=16 * 2 ** 20),
        name="legendre_sums",
    )(assignment.reshape(1, -1), degree, legendre, coefficients)


def synthesis_kernel(spectra_ref, place_ref, table_ref, out_ref, buffer, semaphore):
    wave_count, size = spectra_ref.shape[:2]
    rows, padded = place_ref.shape
    row_count = rows // wave_count
    items = size // row_count
    spectra = spectra_ref[...].astype(jnp.float32)
    placed = []
    for i in range(items):
        item = spectra[:, i * row_count:(i + 1) * row_count].reshape(rows, 2 * C).astype(jnp.bfloat16)
        placed.append(lax.dot_general(
            item, place_ref[...], (((0,), (0,)), ((), ())), preferred_element_type=jnp.float32
        ).astype(jnp.bfloat16))

    def part(half, item, block):
        return placed[item][half * C:(half + 1) * C, block * LANES:(block + 1) * LANES]

    def rows_of(blocks):
        return jnp.concatenate([jnp.concatenate([f(i) for f in blocks], axis=1) for i in range(items)], axis=0)

    even = jnp.concatenate([
        rows_of([lambda i: part(0, i, 0), lambda i: part(0, i, 1), lambda i: part(1, i, 0), lambda i: part(1, i, 1)]),
        rows_of([lambda i: part(0, i, 0), lambda i: -part(0, i, 1), lambda i: part(1, i, 0), lambda i: -part(1, i, 1)]),
    ], axis=0)
    odd = jnp.concatenate([
        rows_of([lambda i: part(0, i, 2), lambda i: part(0, i, 3), lambda i: part(1, i, 2), lambda i: part(1, i, 3)]),
        rows_of([lambda i: -part(1, i, 2), lambda i: part(1, i, 3), lambda i: part(0, i, 2), lambda i: -part(0, i, 3)]),
    ], axis=0)
    chunks = QUARTER // CHUNK

    def copy(n, q):
        return pltpu.make_async_copy(
            buffer.at[n, q],
            out_ref.at[0, :, :, pl.ds(q * QUARTER + n * CHUNK, CHUNK)],
            semaphore.at[n, q],
        )

    for n in range(chunks):
        columns = slice(n * CHUNK, (n + 1) * CHUNK)
        from_even = jnp.dot(even, table_ref[:padded, columns], preferred_element_type=jnp.float32)
        from_odd = jnp.dot(odd, table_ref[padded:, columns], preferred_element_type=jnp.float32)
        buffer[n, :2] = (from_even + from_odd).reshape(2, items, C, CHUNK)
        buffer[n, 2:] = (from_even - from_odd).reshape(2, items, C, CHUNK)
        for q in range(4):
            copy(n, q).start()
    for n in range(chunks):
        for q in range(4):
            copy(n, q).wait()


def synthesis(spectra, place, table):
    items = spectra.shape[0] * spectra.shape[1] // place.shape[0]
    chunks = QUARTER // CHUNK
    return pl.pallas_call(
        synthesis_kernel,
        out_shape=jax.ShapeDtypeStruct((1, items, C, LONGITUDES), jnp.float32),
        in_specs=[pl.BlockSpec(memory_space=pltpu.VMEM)] * 3,
        out_specs=pl.BlockSpec(memory_space=pl.ANY),
        scratch_shapes=[
            pltpu.VMEM((chunks, 4, items, C, CHUNK), jnp.float32),
            pltpu.SemaphoreType.DMA((chunks, 4)),
        ],
        cost_estimate=pl.CostEstimate(flops=10 ** 9, bytes_accessed=6 * 10 ** 6, transcendentals=0),
        compiler_params=pltpu.CompilerParams(vmem_limit_bytes=24 * 2 ** 20),
        name="synthesis",
    )(spectra, place, table)


def shards(legendre, coefficients, assignment):
    wave_count = lax.axis_size("wave")
    ring = [2 * y + core for y in Y_ORDER for core in range(2)]
    gathered = lax.all_gather(coefficients, "lat", axis=1, tiled=True, axis_index_groups=[ring])
    degree = degree_row(legendre.shape[1], gathered)
    degree, assignment = lax.optimization_barrier((degree, assignment))
    by_dest, place = legendre_sums(assignment, degree, jnp.swapaxes(legendre, 1, 2), gathered, wave_count)
    exchanged = lax.all_to_all(
        by_dest, "wave", split_axis=0, concat_axis=0, tiled=True, axis_index_groups=[wave_order(wave_count)]
    )
    table = synthesis_table(MTOP - assignment.shape[0] + 1, assignment.shape[0])
    return synthesis(exchanged, place, table)


def solution(mesh):
    in_specs = (P("wave", None, "lat"), P("wave", "lat", None), P())
    out_specs = P("lat", "wave", None, None)
    return jax.shard_map(shards, mesh=mesh, in_specs=in_specs, out_specs=out_specs, check_vma=False)
```
